256 devices in a mesh: dp: 32 (over z, x), ctx: 2 (over core), tp: 4 (over y).
Axes of the slice: x: 4, y: 4, z: 8, core: 2. Of those that a mesh axis runs over, the one named last changes fastest.
Arguments:
- head_inputs: bfloat16 [32768, 8192], P(('dp', 'ctx'), 'tp'), may hold values from -6 to 6
- write_vecs: bfloat16 [32768, 1024], P(('dp', 'ctx'), 'tp'), may hold values from -6 to 6
- read_vecs: bfloat16 [32768, 1024], P(('dp', 'ctx'), 'tp'), may hold values from -6 to 6
- step_raw: bfloat16 [32768, 128], P(('dp', 'ctx'), 'tp'), may hold values from -8 to 5
- decay_log: float32 [128], P('tp'), may hold values from -5 to 2.5
- step_bias: float32 [128], P('tp'), may hold values from -0.5 to 0.5
- skip_gain: float32 [128], P('tp'), may hold values from 0.5 to 1.5
- out_cotangent: bfloat16 [32768, 8192], P(('dp', 'ctx'), 'tp'), may hold values from -6 to 6
- rollout_lengths: int32 [32, 3], P('dp'), may hold values from 1 to 512, 1024 in all within a row
- plan_place: int32 [32768], P(('dp', 'ctx')), may hold values from 0 to 32767, as said below
- plan_anchor: int32 [32768], P(('dp', 'ctx')), may hold values from 0 to 32767, as said below
Outputs:
- layer_out: bfloat16 [32768, 8192], P(('dp', 'ctx'), 'tp')
- grad_inputs: bfloat16 [32768, 8192], P(('dp', 'ctx'), 'tp')
- grad_write: bfloat16 [32768, 1024], P(('dp', 'ctx'), 'tp')
- grad_read: bfloat16 [32768, 1024], P(('dp', 'ctx'), 'tp')
- grad_step: bfloat16 [32768, 128], P(('dp', 'ctx'), 'tp')
- param_grads: float32 [3, 128], P(None, 'tp')
The draws below stay inside these ranges and needn't reach their ends.
Inputs may be any that keep to these rules, and one draw needn't show every extreme that they name: `plan_place`: all values distinct; the rows that one generator device sends to one device number at most 16, exactly 16 for some pairs; every device receives 512 rows; the lists of counts from each generator device to the 64 devices are rearrangements of one list. `plan_anchor`: the inverse of plan_place.
All inputs are finite; a program needn't handle non-finite values.
Results may differ from the reference program's by a relative error of at most 0.0039.
Values may be sent and summed in bfloat16 or wider, within the bound.
A program may use at most 128 MiB of HBM per device.

```python
import math
import jax
import jax.numpy as jnp
import numpy as np
from jax import lax

SELECTIVE_SHARE = 128
GROUPS = 4
HEAD = 64
STATE = 256
BLOCK = 256
NDOC = 3
TOK_DEV = 512
NGEN = 64
ENTRY_COUNT_ALL = 32768
SEQ = 1024
N_DP = 32
N_CTX = 2


def plan_tables(key):
    average = TOK_DEV // NGEN
    half_count = NGEN // 2
    derived_seed_keys = jax.random.split(key, 5)
    swings = jax.random.randint(derived_seed_keys[0], (half_count,), 0, average + 1)
    swings = swings.at[0].set(average)
    counts = jnp.concatenate([average + swings, average - swings]).astype(jnp.int32)
    counts = counts[jax.random.permutation(derived_seed_keys[1], NGEN)]
    shifts = jax.random.permutation(derived_seed_keys[2], NGEN)
    labels = jax.random.permutation(derived_seed_keys[3], NGEN)
    unlabel = jnp.argsort(labels)
    target_off = jnp.cumsum(counts) - counts
    row_ids = jnp.arange(TOK_DEV, dtype=jnp.int32)

    def one_source(source):
        piece_order = jax.random.permutation(jax.random.fold_in(derived_seed_keys[4], source), NGEN)
        ordered = counts[piece_order]
        ordered_off = jnp.cumsum(ordered) - ordered
        source_off = jnp.zeros((NGEN,), jnp.int32).at[piece_order].set(ordered_off.astype(jnp.int32))
        target = labels[(unlabel[source] + shifts) % NGEN]
        inside = (row_ids[:, None] >= source_off[None, :]) & (row_ids[:, None] < (source_off + counts)[None, :])
        piece_idx = jnp.argmax(inside.astype(jnp.int32), axis=1)
        return target[piece_idx] * TOK_DEV + target_off[piece_idx] + row_ids - source_off[piece_idx]
    places = jax.vmap(one_source)(jnp.arange(NGEN, dtype=jnp.int32)).reshape(ENTRY_COUNT_ALL).astype(jnp.int32)
    anchor = jnp.zeros((ENTRY_COUNT_ALL,), jnp.int32).at[places].set(jnp.arange(ENTRY_COUNT_ALL, dtype=jnp.int32))
    return (places, anchor)


def draw_plan_place(key, part):
    places, anchor = plan_tables(key)
    return places


def draw_plan_anchor(key, part):
    places, anchor = plan_tables(key)
    return anchor


def draw_decay_log(key, part):
    key = jax.random.fold_in(key, 21)
    values = jax.random.uniform(key, (SELECTIVE_SHARE,), jnp.float32, -4.5, 2.5)
    return values


def draw_step_raw(key, part):
    key = jax.random.fold_in(key, 22)
    derived_seed_keys = jax.random.split(key, 3)
    initial_displacement = -5.0 + 0.7 * jax.random.truncated_normal(derived_seed_keys[0], -3.0, 3.0, (ENTRY_COUNT_ALL, SELECTIVE_SHARE), jnp.float32)
    contiguous_extent = jax.random.bernoulli(derived_seed_keys[1], 1.0 / 512.0, (ENTRY_COUNT_ALL, SELECTIVE_SHARE))
    raised_quantity = jax.random.uniform(derived_seed_keys[2], (ENTRY_COUNT_ALL, SELECTIVE_SHARE), jnp.float32, 3.5, 4.5)
    return jnp.where(contiguous_extent, raised_quantity, initial_displacement).astype(jnp.bfloat16)


def shard_levels(rng, shape, cuts, least, top_value):
    level, own = 1.0, jax.random.fold_in(rng, 6)
    for dim, shards_of in cuts:
        steps = jnp.exp(jax.random.uniform(jax.random.fold_in(own, dim), (shards_of,), jnp.float32, least / len(cuts), top_value / len(cuts)))
        level = level * jnp.repeat(steps, shape[dim] // shards_of).reshape([-1 if axis == dim else 1 for axis in range(len(shape))])
    return level


def split_up(amount, total, reach, slope):
    portions = [(1 << 20) // math.isqrt(grade ** slope) + 1 for grade in range(2, amount + 1)]
    surplus, given = total - reach - (amount - 1), [1] * (amount - 1)
    while surplus > 0:
        candidates = [i for i in range(amount - 1) if given[i] < reach]
        pool, left = sum([portions[i] for i in candidates]), surplus
        for i in candidates:
            extra = min(reach - given[i], max(1, left * portions[i] // pool), surplus)
            given[i] = given[i] + extra
            surplus = surplus - extra
    return np.array([reach] + given)


def uneven(key, number_of, total, bound, skew):
    if number_of == 2:
        one = jax.random.randint(key, (), max(1, total - bound), min(bound, total - 1) + 1)
        return jnp.stack([one, total - one])
    lengths = jnp.asarray(split_up(number_of, total, bound, skew), jnp.int32)
    pairs = (number_of - 1) // 2
    source_of, receiver = lengths[1:1 + 2 * pairs:2], lengths[2:2 + 2 * pairs:2]
    margin = jnp.minimum(source_of - 1, bound - receiver)
    shifted = jax.random.randint(jax.random.fold_in(key, 1), (pairs,), 0, 1 << 20) % (margin + 1)
    lengths = lengths.at[1:1 + 2 * pairs:2].set(source_of - shifted).at[2:2 + 2 * pairs:2].set(receiver + shifted)
    return lengths[jax.random.permutation(jax.random.fold_in(key, 2), number_of)]


def centred(own_key, shape, deviation, limit, cuts=(), kind=jnp.bfloat16):
    values = deviation * jax.random.normal(own_key, shape, jnp.float32)
    if cuts:
        values = values * shard_levels(own_key, shape, cuts, -0.22, 0.18)
    return jnp.clip(values, -limit, limit).astype(kind)


def setup_inputs(seed: int = 0) -> dict:
    keys = jax.random.split(jax.random.key(seed), 12)
    return {
        "head_inputs": centred(keys[0], (ENTRY_COUNT_ALL, SELECTIVE_SHARE * HEAD), 1.0, 6.0, ((0, 64), (1, 4))),
        "write_vecs": centred(keys[1], (ENTRY_COUNT_ALL, GROUPS * STATE), 1.0, 6.0, ((0, 64), (1, 4))),
        "read_vecs": centred(keys[2], (ENTRY_COUNT_ALL, GROUPS * STATE), 1.0, 6.0, ((0, 64), (1, 4))),
        "step_raw": draw_step_raw(jax.random.fold_in(keys[11], 71), 0),
        "decay_log": draw_decay_log(jax.random.fold_in(keys[11], 71), 0),
        "step_bias": jnp.clip(jax.random.uniform(keys[5], (SELECTIVE_SHARE,), jnp.float32, -0.5, 0.5) * shard_levels(keys[5], (SELECTIVE_SHARE,), ((0, 4),), -0.4, 0.0), -0.5, 0.5),
        "skip_gain": jnp.clip(0.5 + 1.0 * jax.random.uniform(keys[6], (SELECTIVE_SHARE,), jnp.float32) ** shard_levels(keys[6], (SELECTIVE_SHARE,), ((0, 4),), -0.2, 0.2), 0.5, 1.5),
        "out_cotangent": centred(keys[7], (ENTRY_COUNT_ALL, SELECTIVE_SHARE * HEAD), 1.0, 6.0, ((0, 64), (1, 4))),
        "rollout_lengths": jax.vmap(lambda own: uneven(own, NDOC, SEQ, SEQ // 2, 0))(jax.random.split(keys[8], N_DP)).reshape((N_DP, NDOC)).astype(jnp.int32),
        "plan_place": draw_plan_place(jax.random.fold_in(keys[11], 71), 0),
        "plan_anchor": draw_plan_anchor(jax.random.fold_in(keys[11], 71), 0),
    }


PRECISE = lax.Precision.HIGHEST

def block_step(carry_state, pieces, decay_rate, gain_vals):
    head_rows, write_rows, read_rows, step_size, starts = pieces
    row_count = head_rows.shape[0]
    attention_unit_number = step_size.shape[1]
    group_count = write_rows.shape[1] // STATE
    per_group = attention_unit_number // group_count
    head_vals = head_rows.astype(jnp.float32).reshape(row_count, group_count, per_group, HEAD)
    write_grp = write_rows.astype(jnp.float32).reshape(row_count, group_count, STATE)
    read_grp = read_rows.astype(jnp.float32).reshape(row_count, group_count, STATE)
    running = jnp.cumsum(step_size * decay_rate[None, :], axis=0)
    segment = jnp.cumsum(starts)
    row_index = jnp.arange(row_count)
    same_seg = (segment[:, None] == segment[None, :]) & (row_index[:, None] >= row_index[None, :])
    running_heads = running.T
    gaps = running_heads[:, :, None] - running_heads[:, None, :]
    decay_mat = jnp.where(same_seg[None], jnp.exp(jnp.where(same_seg[None], gaps, 0.0)), 0.0)
    intersection = jnp.einsum('tgn,sgn->gts', read_grp, write_grp, precision=PRECISE)
    scores = intersection[:, None] * decay_mat.reshape(group_count, per_group, row_count, row_count) * step_size.T.reshape(group_count, per_group, 1, row_count)
    inner_part = jnp.einsum('gjts,sgjp->tgjp', scores, head_vals, precision=PRECISE)
    entering = jnp.exp(running) * (segment == 0)[:, None]
    state_four = carry_state.reshape(group_count, per_group, HEAD, STATE)
    carried = jnp.einsum('tgn,gjpn->tgjp', read_grp, state_four, precision=PRECISE)
    output = inner_part + entering.reshape(row_count, group_count, per_group, 1) * carried + gain_vals.reshape(1, group_count, per_group, 1) * head_vals
    leaving = jnp.exp(running[-1][None, :] - running) * (segment == segment[-1])[:, None]
    keeping = jnp.exp(running[-1]) * (segment[-1] == 0)
    weighted = (leaving * step_size).reshape(row_count, group_count, per_group, 1) * head_vals
    fresh_state = jnp.einsum('sgjp,sgn->gjpn', weighted, write_grp, precision=PRECISE)
    new_state = fresh_state + keeping.reshape(group_count, per_group, 1, 1) * state_four
    return (new_state.reshape(attention_unit_number, HEAD, STATE), output.reshape(row_count, attention_unit_number * HEAD))

def run_blocks(head_rows, write_rows, read_rows, step_rows, log_decay, bias_vals, gain_vals, starts, first_state):
    row_count = head_rows.shape[0]
    block_count = row_count // BLOCK
    step_size = jax.nn.softplus(step_rows.astype(jnp.float32) + bias_vals[None, :])
    decay_rate = -jnp.exp(log_decay)

    def advance(carry_state, pieces):
        return jax.checkpoint(block_step)(carry_state, pieces, decay_rate, gain_vals)
    pieces = (head_rows.reshape(block_count, BLOCK, -1), write_rows.reshape(block_count, BLOCK, -1), read_rows.reshape(block_count, BLOCK, -1), step_size.reshape(block_count, BLOCK, -1), starts.reshape(block_count, BLOCK))
    final_state, outputs = lax.scan(advance, first_state, pieces)
    return (outputs.reshape(row_count, -1), final_state)

def reference(head_inputs, write_vecs, read_vecs, step_raw, decay_log, step_bias, skip_gain, out_cotangent, rollout_lengths, plan_place, plan_anchor):
    seq_rows = TOK_DEV * N_CTX

    def packed(values):
        return values[plan_anchor].reshape(N_DP, seq_rows, values.shape[1])
    inputs = packed(head_inputs)
    writes = packed(write_vecs)
    read_rows = packed(read_vecs)
    step_rows = packed(step_raw)
    cotangent = out_cotangent.reshape(N_DP, seq_rows, -1)
    bounds = jnp.cumsum(rollout_lengths, axis=1) - rollout_lengths
    position = jnp.arange(seq_rows, dtype=jnp.int32)
    starts = jnp.any(position[None, :, None] == bounds[:, None, :], axis=2).astype(jnp.int32)
    zero_state = jnp.zeros((SELECTIVE_SHARE, HEAD, STATE), jnp.float32)

    def one_group(group_data):
        head_grp, write_grp, read_grp, step_grp, start_group, cot_grp = group_data

        def forward(head_arg, write_arg, read_arg, step_arg, decay_arg, bias_arg, gain_arg):
            return run_blocks(head_arg, write_arg, read_arg, step_arg, decay_arg, bias_arg, gain_arg, start_group, zero_state)[0]
        output, pullback = jax.vjp(forward, head_grp, write_grp, read_grp, step_grp, decay_log, step_bias, skip_gain)
        gradients = pullback(cot_grp.astype(jnp.float32))
        return (output.astype(jnp.bfloat16),) + tuple(gradients)
    results = lax.map(one_group, (inputs, writes, read_rows, step_rows, starts, cotangent))
    layer_out = results[0].reshape(ENTRY_COUNT_ALL, -1)

    def unpack(values):
        return values.reshape(ENTRY_COUNT_ALL, -1)[plan_place]
    factor = 1.0 / math.sqrt(ENTRY_COUNT_ALL * HEAD)
    param_grads = jnp.stack([lax.optimization_barrier(jnp.sum(results[5], axis=0)), lax.optimization_barrier(jnp.sum(results[6], axis=0)), lax.optimization_barrier(jnp.sum(results[7], axis=0))]) * factor
    return (layer_out, unpack(results[1]), unpack(results[2]), unpack(results[3]), unpack(results[4]), param_grads)
```

```python
import math

import jax
import jax.numpy as jnp
from jax import lax
from jax.experimental import pallas as pl
from jax.experimental.pallas import tpu as pltpu
from jax.sharding import PartitionSpec as P

HEAD = 64
STATE = 256
BLOCK = 256
ROWS = 512
HEADS = 32
WIDTH = HEADS * HEAD
PEERS = 64
CAP = 16
SLOTS = PEERS * CAP
SMALL = 2 * STATE + 128
CHUNKS = 4
CHUNK = WIDTH // CHUNKS
MESH = pl.DeviceIdType.MESH
F32 = jnp.float32
BF16 = jnp.bfloat16
PRECISE = lax.Precision.HIGHEST


def nn(a, b, **kw):
    return lax.dot_general(a, b, (((1,), (0,)), ((), ())), preferred_element_type=F32, **kw)


def nt(a, b):
    return lax.dot_general(a, b, (((1,), (1,)), ((), ())), preferred_element_type=F32)


def tn(a, b):
    return lax.dot_general(a, b, (((0,), (0,)), ((), ())), preferred_element_type=F32)


def split(v):
    high = v.astype(BF16)
    return high, (v - high.astype(F32)).astype(BF16)


def both(product, a, b):
    if isinstance(a, tuple) and isinstance(b, tuple):
        return product(a[0], b[0]) + product(a[0], b[1]) + product(a[1], b[0])
    if isinstance(a, tuple):
        return product(a[0], b) + product(a[1], b)
    return product(a, b[0]) + product(a, b[1])


def iota(shape, dim):
    return lax.broadcasted_iota(jnp.int32, shape, dim)


def as_bf16(mask):
    return mask.astype(F32).astype(BF16)


def column(row):
    n = row.shape[1]
    return jnp.sum(jnp.where(iota((n, n), 0) == iota((n, n), 1), row, jnp.zeros((), row.dtype)), axis=1, keepdims=True)


def int_column(row):
    return column(row.astype(F32)).astype(jnp.int32)


def split_heads(ref, values, part=slice(None)):
    for h in range(HEADS):
        ref[h, :, part] = values[h : h + 1, :]


def join_heads(ref, part=slice(None)):
    return jnp.concatenate([ref[h, :, part] for h in range(HEADS)], axis=0)


def send_slot_row(place_row):
    target = lax.shift_right_logical(place_row, 9)
    ids = iota((PEERS, ROWS), 0)
    match = ids == target
    earlier = as_bf16(iota((ROWS, ROWS), 0) < iota((ROWS, ROWS), 1))
    before = nn(as_bf16(match), earlier)
    slot = jnp.sum(jnp.where(match, before + (ids * CAP).astype(F32), 0.0), axis=0, keepdims=True)
    return slot.astype(jnp.int32)


def send_slot_col(place_col):
    target = lax.shift_right_logical(place_col, 9)
    ids = iota((ROWS, PEERS), 1)
    match = ids == target
    earlier = as_bf16(iota((ROWS, ROWS), 1) < iota((ROWS, ROWS), 0))
    before = nn(earlier, as_bf16(match))
    slot = jnp.sum(jnp.where(match, before + (ids * CAP).astype(F32), 0.0), axis=1, keepdims=True)
    return slot.astype(jnp.int32)


def take_slot_row(anchor_col, anchor_row):
    source_row = lax.shift_right_logical(anchor_row, 9)
    same = lax.shift_right_logical(anchor_col, 9) == source_row
    before = jnp.where(same & (anchor_col < anchor_row), 1.0, 0.0)
    return source_row * CAP + jnp.sum(before, axis=0, keepdims=True).astype(jnp.int32)


def take_slot_col(anchor_col, anchor_row):
    source_col = lax.shift_right_logical(anchor_col, 9)
    same = source_col == lax.shift_right_logical(anchor_row, 9)
    before = jnp.where(same & (anchor_row < anchor_col), 1.0, 0.0)
    return source_col * CAP + jnp.sum(before, axis=1, keepdims=True).astype(jnp.int32)


def softplus(v):
    return jnp.maximum(v, 0.0) + jnp.log1p(jnp.exp(-jnp.abs(v)))


def starts_between(len_ref, low, high):
    first = len_ref[0, 0]
    second = first + len_ref[0, 1]
    count = jnp.zeros(jnp.broadcast_shapes(jnp.shape(low), jnp.shape(high)), F32)
    for bound in (0, first, second):
        count = count + jnp.where((bound >= low) & (bound <= high), 1.0, 0.0)
    return count


def running_sum(rate):
    upto = (iota((BLOCK, BLOCK), 0) <= iota((BLOCK, BLOCK), 1)).astype(F32)
    return nn(rate, upto, precision=PRECISE)


def peer_copies(me, source, target, send_sem, recv_sem):
    @pl.loop(1, PEERS)
    def _(k):
        peer = lax.rem(me + k, PEERS)
        pltpu.make_async_remote_copy(
            src_ref=source.at[pl.ds(pl.multiple_of(peer * CAP, CAP), CAP)],
            dst_ref=target.at[pl.ds(pl.multiple_of(me * CAP, CAP), CAP)],
            send_sem=send_sem,
            recv_sem=recv_sem,
            device_id={"dp": peer // 2, "ctx": lax.rem(peer, 2)},
            device_id_type=MESH,
        ).start()

    own = pl.ds(pl.multiple_of(me * CAP, CAP), CAP)
    target[own, :] = source[own, :]


def wait_peers(ref, sem):
    view = ref.at[pl.ds(0, SLOTS - CAP)]
    pltpu.make_async_copy(view, view, sem).wait()


def layer_kernel(
    len_ref, place_ref, anchor_ref,
    x_ref, w_ref, r_ref, s_ref, cot_ref, dec_ref, bias_ref, skip_ref,
    y_ref, gx_ref, gw_ref, gr_ref, gs_ref, par_ref,
    snd_s, snd_x, lnd_s, lnd_x, bck_s, bck_x, ret_s, ret_x, edge_out, edge_in,
    perm_ref, pick_ref, xt_ref, bc_ref, u_ref, scale_ref, gain_ref,
    run_ref, wide_ref, step_ref, ent_ref, lev_ref, keep_ref, mask_ref, gram_ref, dgram_ref,
    dw_ref, dr_ref, dx_ref, yy_ref, xi_ref, xs_ref, kd_ref, gg_ref, dbc_ref,
    send_sem, recv_sem, back_send_sem, back_recv_sem, edge_send_sem, edge_recv_sem,
):
    dp, ctx = lax.axis_index("dp"), lax.axis_index("ctx")
    me = dp * 2 + ctx
    barrier = pltpu.get_barrier_semaphore()

    @pl.loop(1, PEERS)
    def _(k):
        peer = lax.rem(me + k, PEERS)
        pl.semaphore_signal(
            barrier, inc=1, device_id={"dp": peer // 2, "ctx": lax.rem(peer, 2)}, device_id_type=MESH
        )

    perm_ref[...] = as_bf16(iota((SLOTS, ROWS), 0) == send_slot_row(place_ref[...]))
    snd_s[:, :STATE] = nn(perm_ref[...], w_ref[...]).astype(BF16)
    snd_s[:, STATE : 2 * STATE] = nn(perm_ref[...], r_ref[...]).astype(BF16)
    steps = jnp.concatenate([s_ref[...], jnp.zeros((128 - HEADS, ROWS), BF16)], axis=0)
    snd_s[:, 2 * STATE :] = nt(perm_ref[...], steps).astype(BF16)
    pl.semaphore_wait(barrier, PEERS - 1)
    peer_copies(me, snd_s, lnd_s, send_sem.at[CHUNKS], recv_sem.at[CHUNKS])
    for k in range(CHUNKS):
        for half in range(CHUNK // 256):
            inside = slice(half * 256, half * 256 + 256)
            cols = slice(k * CHUNK + half * 256, k * CHUNK + half * 256 + 256)
            snd_x[k, :, inside] = nn(perm_ref[...], x_ref[:, cols]).astype(BF16)
        peer_copies(me, snd_x.at[k], lnd_x.at[k], send_sem.at[k], recv_sem.at[k])

    base = ctx * ROWS
    is_late = (ctx == 1).astype(F32)
    is_early = (ctx == 0).astype(F32)
    parts = (slice(0, BLOCK), slice(BLOCK, 2 * BLOCK))
    anchor_row, anchor_col = anchor_ref[...], int_column(anchor_ref[...])
    take_r = take_slot_row(anchor_col, anchor_row)
    pick_ref[...] = as_bf16(iota((SLOTS, ROWS), 0) == take_r)
    take_c = take_slot_col(anchor_col, anchor_row)
    pick = as_bf16(iota((ROWS, SLOTS), 1) == take_c)

    wait_peers(lnd_s, recv_sem.at[CHUNKS])
    bc_ref[...] = nn(pick, lnd_s[:, : 2 * STATE]).astype(BF16)
    u_ref[...] = tn(lnd_s[:, 2 * STATE :], pick_ref[...])[:HEADS] + column(bias_ref[...])
    u = u_ref[...]
    step = softplus(u)
    decay = -jnp.exp(column(dec_ref[...]))
    split_heads(gain_ref, jnp.broadcast_to(column(skip_ref[...]), (HEADS, BLOCK)))
    rate = decay * step
    split_heads(step_ref, step)
    keeps, runs = [], []
    for c in range(2):
        part = parts[c]
        first = base + c * BLOCK
        last = first + BLOCK - 1
        run = running_sum(rate[:, part])
        runs.append(run)
        split_heads(run_ref, run, part)
        pos = first + iota((1, BLOCK), 1)
        pos_col = first + iota((BLOCK, 1), 0)
        open_start = (starts_between(len_ref, jnp.full((1, BLOCK), first, jnp.int32), pos) == 0).astype(F32)
        open_end = (starts_between(len_ref, pos + 1, jnp.full((1, BLOCK), last, jnp.int32)) == 0).astype(F32)
        run_end = run[:, BLOCK - 1 :]
        split_heads(ent_ref, jnp.exp(run) * open_start, part)
        split_heads(lev_ref, jnp.exp(run_end - run) * step[:, part] * open_end, part)
        kept = jnp.exp(run_end) * open_start[:, BLOCK - 1 :]
        keeps.append(kept)
        split_heads(keep_ref, jnp.broadcast_to(kept, (HEADS, BLOCK)), part)
        crossing = starts_between(len_ref, pos + 1, pos_col)
        mask_ref[c] = jnp.where((pos_col >= pos) & (crossing == 0), 0.0, -1e30)
        tall = jnp.concatenate([run, jnp.zeros((128 - HEADS, BLOCK), F32)], axis=0).T
        for h in range(HEADS):
            wide_ref[h, part, :] = jnp.broadcast_to(tall[:, h : h + 1], (BLOCK, 128))
        gram_ref[c] = nt(bc_ref[part, STATE:], bc_ref[part, :STATE])
        dgram_ref[c] = jnp.zeros((BLOCK, BLOCK), F32)
        dw_ref[part, :] = jnp.zeros((BLOCK, STATE), F32)
        dr_ref[part, :] = jnp.zeros((BLOCK, STATE), F32)

    whole = jnp.concatenate([runs[0], runs[1] + runs[0][:, BLOCK - 1 :]], axis=1)
    pos = base + iota((1, ROWS), 1)
    open_end = (starts_between(len_ref, pos + 1, jnp.full((1, ROWS), base + ROWS - 1, jnp.int32)) == 0).astype(F32)
    open_start = (starts_between(len_ref, jnp.full((1, ROWS), base, jnp.int32), pos) == 0).astype(F32)
    leave_all = jnp.exp(whole[:, ROWS - 1 :] - whole) * step * open_end
    enter_all = jnp.exp(whole) * open_start
    split_heads(scale_ref, is_early * leave_all + is_late * enter_all)

    def scaled(h, values):
        four = [values[HEAD * i : HEAD * i + HEAD] * scale_ref[h + i] for i in range(4)]
        return split(jnp.concatenate(four, axis=0))

    def edge_copy(k):
        return pltpu.make_async_remote_copy(
            src_ref=edge_out.at[k],
            dst_ref=edge_in.at[k],
            send_sem=edge_send_sem.at[k],
            recv_sem=edge_recv_sem.at[k],
            device_id={"dp": dp, "ctx": 1 - ctx},
            device_id_type=MESH,
        )

    def open_chunk(k):
        wait_peers(lnd_x.at[k], recv_sem.at[k])
        for q in range(CHUNK // 256):
            inside = slice(q * 256, q * 256 + 256)
            rows = slice(k * CHUNK + q * 256, k * CHUNK + q * 256 + 256)
            xt_ref[rows, :] = tn(lnd_x[k, :, inside], pick_ref[...]).astype(BF16)
        head = k * CHUNK // HEAD

        @pl.when(ctx == 0)
        def _():
            for q in range(CHUNK // 256):
                rows = slice(k * CHUNK + q * 256, k * CHUNK + q * 256 + 256)
                values = scaled(head + 4 * q, xt_ref[rows, :].astype(F32))
                edge_out[k, q * 256 : q * 256 + 256, :] = both(nn, values, bc_ref[:, :STATE])

        @pl.when(ctx == 1)
        def _():
            for q in range(CHUNK // 256):
                rows = slice(k * CHUNK + q * 256, k * CHUNK + q * 256 + 256)
                values = scaled(head + 4 * q, cot_ref[:, rows].astype(F32).T)
                edge_out[k, q * 256 : q * 256 + 256, :] = both(nn, values, bc_ref[:, STATE:])

        edge_copy(k).start()

    def rows_of(ref, j, part):
        return jnp.concatenate(
            [jnp.broadcast_to(ref[2 * j + i, :, part], (HEAD, BLOCK)) for i in range(2)], axis=0
        )

    def pair(k, near):
        j = k * (CHUNK // 128) + near
        rows = pl.ds(pl.multiple_of(j * 128, 128), 128)
        edge = edge_in[k, pl.ds(pl.multiple_of(near * 128, 128), 128), :]
        x_t = [xt_ref[rows, part] for part in parts]
        x_f = [v.astype(F32) for v in x_t]
        d_n = [cot_ref[part, rows] for part in parts]
        d_f = [v.astype(F32).T for v in d_n]
        d_t = [v.astype(BF16) for v in d_f]
        gain = rows_of(gain_ref, j, slice(None))
        ent = [rows_of(ent_ref, j, part) for part in parts]
        lev = [rows_of(lev_ref, j, part) for part in parts]
        keep = [rows_of(keep_ref, j, part) for part in parts]
        w_t = [split(x_f[c] * lev[c]) for c in range(2)]
        v_t = [split(d_f[c] * ent[c]) for c in range(2)]
        state0 = edge * is_late
        state1 = both(nn, w_t[0], bc_ref[parts[0], :STATE]) + keep[0] * state0
        grad1 = edge * is_early
        grad0 = both(nn, v_t[1], bc_ref[parts[1], STATE:]) + keep[1] * grad1
        states, grads = (state0, state1), (grad0, grad1)
        upper = iota((128, BLOCK), 0) < HEAD
        for c in range(2):
            part = parts[c]
            y_parts, dx_parts = [], []
            for i in range(2):
                own = slice(HEAD * i, HEAD * i + HEAD)
                tall = wide_ref[2 * j + i, part, :]
                gap = jnp.concatenate([tall, tall], axis=1) - run_ref[2 * j + i, :, part]
                decayed = jnp.exp(gap + mask_ref[c]) * step_ref[2 * j + i, :, part]
                scores = split(gram_ref[c] * decayed)
                y_parts.append(both(nt, x_t[c][own], scores))
                dx_parts.append(both(nn, d_t[c][own], scores))
                only = jnp.where(upper if i == 0 else jnp.logical_not(upper), x_f[c], 0.0).astype(BF16)
                dgram_ref[c] += nn(d_n[c], only) * decayed
            state_b, grad_b = split(states[c]), split(grads[c])
            y_f = jnp.concatenate(y_parts, axis=0) + both(nt, state_b, bc_ref[part, STATE:]) * ent[c]
            dx_i = jnp.concatenate(dx_parts, axis=0)
            dx_s = both(nt, grad_b, bc_ref[part, :STATE]) * lev[c]
            yy, xi, xs, gg = d_f[c] * y_f, x_f[c] * dx_i, x_f[c] * dx_s, x_f[c] * d_f[c]
            kd = states[c] * grads[c]
            for i in range(2):
                own = slice(HEAD * i, HEAD * i + HEAD)
                one = 2 * j + i
                yy_ref[one, :, part] = jnp.sum(yy[own], axis=0, keepdims=True)
                xi_ref[one, :, part] = jnp.sum(xi[own], axis=0, keepdims=True)
                xs_ref[one, :, part] = jnp.sum(xs[own], axis=0, keepdims=True)
                gg_ref[one, :, part] = jnp.sum(gg[own], axis=0, keepdims=True)
                kd_ref[one, :, part] = jnp.sum(kd[own], axis=0, keepdims=True)
            y_ref[part, rows] = (y_f + gain * x_f[c]).T.astype(BF16)
            dx_ref[rows, part] = (dx_i + dx_s + gain * d_f[c]).astype(BF16)
            dw_ref[part, :] += both(tn, w_t[c], grad_b)
            dr_ref[part, :] += both(tn, v_t[c], state_b)

    def scan_chunk(k):
        edge_copy(k).wait()

        @pl.loop(0, CHUNK // 128)
        def _(near):
            pair(k, near)

        for q in range(CHUNK // 256):
            inside = slice(q * 256, q * 256 + 256)
            rows = slice(k * CHUNK + q * 256, k * CHUNK + q * 256 + 256)
            bck_x[k, :, inside] = nt(pick_ref[...], dx_ref[rows, :]).astype(BF16)
        peer_copies(me, bck_x.at[k], ret_x.at[k], back_send_sem.at[k], back_recv_sem.at[k])

    for k in range(CHUNKS):
        open_chunk(k)
        if k:
            scan_chunk(k - 1)
    scan_chunk(CHUNKS - 1)

    later = (iota((BLOCK, BLOCK), 0) >= iota((BLOCK, BLOCK), 1)).astype(F32)
    sooner = (iota((BLOCK, BLOCK), 0) < iota((BLOCK, BLOCK), 1)).astype(F32)
    drates = []
    yy, xi, xs = join_heads(yy_ref), join_heads(xi_ref), join_heads(xs_ref)
    for c in range(2):
        part = slice(c * BLOCK, c * BLOCK + BLOCK)
        dg = split(dgram_ref[c])
        write, read = bc_ref[part, :STATE], bc_ref[part, STATE:]
        dbc_ref[part, :STATE] = (dw_ref[part, :] + both(tn, dg, read)).astype(BF16)
        dbc_ref[part, STATE:] = (dr_ref[part, :] + both(nn, dg, write)).astype(BF16)
        through = keeps[c] * jnp.sum(join_heads(kd_ref, part), axis=1, keepdims=True)
        drate = (
            nn(yy[:, part] - xi[:, part], later, precision=PRECISE)
            + nn(xs[:, part], sooner, precision=PRECISE)
            + through
        )
        pos = base + c * BLOCK + iota((1, BLOCK), 1)
        drates.append(drate * (starts_between(len_ref, pos, pos) == 0).astype(F32))
    drate = jnp.concatenate(drates, axis=1)
    dstep = decay * drate + (xi + xs) / step
    du = dstep / (1.0 + jnp.exp(-u))
    lane, head = iota((HEADS, 128), 1), iota((HEADS, 128), 0)
    partial = (
        jnp.where(lane == HEADS + head, jnp.sum(drate * rate, axis=1, keepdims=True), 0.0)
        + jnp.where(lane == 2 * HEADS + head, jnp.sum(du, axis=1, keepdims=True), 0.0)
        + jnp.where(lane == 3 * HEADS + head, jnp.sum(join_heads(gg_ref), axis=1, keepdims=True), 0.0)
    )
    partial = jnp.sum(partial, axis=0, keepdims=True)
    high = partial.astype(BF16).astype(F32)
    middle = (partial - high).astype(BF16).astype(F32)
    low = partial - high - middle
    place = iota((SLOTS, 128), 0) % CAP
    extra = jnp.where(place == 0, high, jnp.where(place == 1, middle, jnp.where(place == 2, low, 0.0)))
    bck_s[:, : 2 * STATE] = nn(pick_ref[...], dbc_ref[...]).astype(BF16)
    du_wide = jnp.concatenate([du, jnp.zeros((128 - HEADS, ROWS), F32)], axis=0).astype(BF16)
    bck_s[:, 2 * STATE :] = (nt(pick_ref[...], du_wide) + extra).astype(BF16)
    peer_copies(me, bck_s, ret_s, back_send_sem.at[CHUNKS], back_recv_sem.at[CHUNKS])

    perm = as_bf16(iota((ROWS, SLOTS), 1) == send_slot_col(int_column(place_ref[...])))
    for k in range(CHUNKS):
        wait_peers(ret_x.at[k], back_recv_sem.at[k])
        for q in range(CHUNK // 256):
            inside = slice(q * 256, q * 256 + 256)
            cols = slice(k * CHUNK + q * 256, k * CHUNK + q * 256 + 256)
            gx_ref[:, cols] = nn(perm, ret_x[k, :, inside]).astype(BF16)
    wait_peers(ret_s, back_recv_sem.at[CHUNKS])
    gw_ref[...] = nn(perm, ret_s[:, :STATE]).astype(BF16)
    gr_ref[...] = nn(perm, ret_s[:, STATE : 2 * STATE]).astype(BF16)
    gs_ref[...] = tn(ret_s[:, 2 * STATE :], perm_ref[...])[:HEADS].astype(BF16)
    total = jnp.sum(ret_s[:, 2 * STATE :].astype(F32), axis=0, keepdims=True)
    par_ref[...] = total * (1.0 / math.sqrt(ROWS * PEERS * HEAD))
    for k in range(CHUNKS):
        wait_peers(snd_x.at[k], send_sem.at[k])
        wait_peers(bck_x.at[k], back_send_sem.at[k])
    wait_peers(snd_s, send_sem.at[CHUNKS])
    wait_peers(bck_s, back_send_sem.at[CHUNKS])


def sds(shape, dtype):
    return jax.ShapeDtypeStruct(shape, dtype)


def vmem(n):
    return [pl.BlockSpec(memory_space=pltpu.VMEM)] * n


def per_device(
    head_inputs, write_vecs, read_vecs, step_raw, decay_log, step_bias, skip_gain,
    out_cotangent, rollout_lengths, plan_place, plan_anchor,
):
    small, large = (SLOTS, SMALL), (CHUNKS, SLOTS, CHUNK)
    per_head = pltpu.VMEM((HEADS, 1, ROWS), F32)
    square = pltpu.VMEM((2, BLOCK, BLOCK), F32)
    transfers = [pltpu.VMEM(shape, BF16) for _ in range(4) for shape in (small, large)]
    edges = [pltpu.VMEM((CHUNKS, CHUNK, STATE), F32)] * 2
    layer_out, grad_x, grad_w, grad_r, grad_s, params = pl.pallas_call(
        layer_kernel,
        out_shape=(
            sds((ROWS, WIDTH), BF16),
            sds((ROWS, WIDTH), BF16),
            sds((ROWS, STATE), BF16),
            sds((ROWS, STATE), BF16),
            sds((HEADS, ROWS), BF16),
            sds((1, 128), F32),
        ),
        in_specs=[pl.BlockSpec(memory_space=pltpu.SMEM)] + vmem(10),
        out_specs=tuple(vmem(6)),
        scratch_shapes=[
            *transfers,
            *edges,
            pltpu.VMEM((SLOTS, ROWS), BF16),
            pltpu.VMEM((SLOTS, ROWS), BF16),
            pltpu.VMEM((WIDTH, ROWS), BF16),
            pltpu.VMEM((ROWS, 2 * STATE), BF16),
            pltpu.VMEM((HEADS, ROWS), F32),
            per_head,
            pltpu.VMEM((HEADS, 1, BLOCK), F32),
            per_head,
            pltpu.VMEM((HEADS, ROWS, 128), F32),
            per_head,
            per_head,
            per_head,
            per_head,
            square,
            square,
            square,
            pltpu.VMEM((ROWS, STATE), F32),
            pltpu.VMEM((ROWS, STATE), F32),
            pltpu.VMEM((WIDTH, ROWS), BF16),
            per_head,
            per_head,
            per_head,
            per_head,
            per_head,
            pltpu.VMEM((ROWS, 2 * STATE), BF16),
            pltpu.SemaphoreType.DMA((CHUNKS + 1,)),
            pltpu.SemaphoreType.DMA((CHUNKS + 1,)),
            pltpu.SemaphoreType.DMA((CHUNKS + 1,)),
            pltpu.SemaphoreType.DMA((CHUNKS + 1,)),
            pltpu.SemaphoreType.DMA((CHUNKS,)),
            pltpu.SemaphoreType.DMA((CHUNKS,)),
        ],
        compiler_params=pltpu.CompilerParams(
            collective_id=0, has_side_effects=True, vmem_limit_bytes=60 * 1024 * 1024
        ),
        name="layer",
    )(
        rollout_lengths, plan_place.reshape(1, ROWS), plan_anchor.reshape(1, ROWS),
        head_inputs, write_vecs, read_vecs, step_raw.T, out_cotangent,
        decay_log.reshape(1, HEADS), step_bias.reshape(1, HEADS), skip_gain.reshape(1, HEADS),
    )
    return (layer_out, grad_x, grad_w, grad_r, grad_s.T, params[0, HEADS:].reshape(3, HEADS))


def solution(mesh):
    rows = P(("dp", "ctx"), "tp")
    return jax.shard_map(
        per_device,
        mesh=mesh,
        in_specs=(
            rows, rows, rows, rows, P("tp"), P("tp"), P("tp"), rows, P("dp", None), P(("dp", "ctx")), P(("dp", "ctx")),
        ),
        out_specs=(rows, rows, rows, rows, rows, P(None, "tp")),
        check_vma=False,
    )
```

```python
import math

import jax
import jax.numpy as jnp
from jax import lax
from jax.experimental import pallas as pl
from jax.experimental.pallas import tpu as pltpu
from jax.sharding import PartitionSpec as P

HEAD = 64
STATE = 256
BLOCK = 256
ROWS = 512
HEADS = 32
WIDTH = HEADS * HEAD
PEERS = 64
CAP = 16
SLOTS = PEERS * CAP
SMALL = 2 * STATE
QUART = CAP // 4
CHUNKS = 4
CHUNK = WIDTH // CHUNKS
MESH = pl.DeviceIdType.MESH
F32 = jnp.float32
BF16 = jnp.bfloat16
PRECISE = lax.Precision.HIGHEST


def nn(a, b, **kw):
    return lax.dot_general(a, b, (((1,), (0,)), ((), ())), preferred_element_type=F32, **kw)


def nt(a, b):
    return lax.dot_general(a, b, (((1,), (1,)), ((), ())), preferred_element_type=F32)


def tn(a, b):
    return lax.dot_general(a, b, (((0,), (0,)), ((), ())), preferred_element_type=F32)


def split(v):
    high = v.astype(BF16)
    return high, (v - high.astype(F32)).astype(BF16)


def both(product, a, b):
    if isinstance(a, tuple) and isinstance(b, tuple):
        return product(a[0], b[0]) + product(a[0], b[1]) + product(a[1], b[0])
    if isinstance(a, tuple):
        return product(a[0], b) + product(a[1], b)
    return product(a, b[0]) + product(a, b[1])


def iota(shape, dim):
    return lax.broadcasted_iota(jnp.int32, shape, dim)


def as_bf16(mask):
    return mask.astype(F32).astype(BF16)


def column(row):
    n = row.shape[1]
    return jnp.sum(jnp.where(iota((n, n), 0) == iota((n, n), 1), row, jnp.zeros((), row.dtype)), axis=1, keepdims=True)


def int_column(row):
    return column(row.astype(F32)).astype(jnp.int32)


def split_heads(ref, values, part=slice(None)):
    for h in range(HEADS):
        ref[h, :, part] = values[h : h + 1, :]


def join_heads(ref, part=slice(None)):
    return jnp.concatenate([ref[h, :, part] for h in range(HEADS)], axis=0)


def send_slot_row(place_row):
    target = lax.shift_right_logical(place_row, 9)
    ids = iota((PEERS, ROWS), 0)
    match = ids == target
    earlier = as_bf16(iota((ROWS, ROWS), 0) < iota((ROWS, ROWS), 1))
    before = nn(as_bf16(match), earlier)
    slot = jnp.sum(jnp.where(match, before + (ids * CAP).astype(F32), 0.0), axis=0, keepdims=True)
    return slot.astype(jnp.int32)


def send_slot_col(place_col):
    target = lax.shift_right_logical(place_col, 9)
    ids = iota((ROWS, PEERS), 1)
    match = ids == target
    earlier = as_bf16(iota((ROWS, ROWS), 1) < iota((ROWS, ROWS), 0))
    before = nn(earlier, as_bf16(match))
    slot = jnp.sum(jnp.where(match, before + (ids * CAP).astype(F32), 0.0), axis=1, keepdims=True)
    return slot.astype(jnp.int32)


def take_slot_row(anchor_col, anchor_row):
    source_row = lax.shift_right_logical(anchor_row, 9)
    same = lax.shift_right_logical(anchor_col, 9) == source_row
    before = jnp.where(same & (anchor_col < anchor_row), 1.0, 0.0)
    return source_row * CAP + jnp.sum(before, axis=0, keepdims=True).astype(jnp.int32)


def take_slot_col(anchor_col, anchor_row):
    source_col = lax.shift_right_logical(anchor_col, 9)
    same = source_col == lax.shift_right_logical(anchor_row, 9)
    before = jnp.where(same & (anchor_row < anchor_col), 1.0, 0.0)
    return source_col * CAP + jnp.sum(before, axis=1, keepdims=True).astype(jnp.int32)


def softplus(v):
    return jnp.maximum(v, 0.0) + jnp.log1p(jnp.exp(-jnp.abs(v)))


def starts_between(len_ref, low, high):
    first = len_ref[0, 0]
    second = first + len_ref[0, 1]
    count = jnp.zeros(jnp.broadcast_shapes(jnp.shape(low), jnp.shape(high)), F32)
    for bound in (0, first, second):
        count = count + jnp.where((bound >= low) & (bound <= high), 1.0, 0.0)
    return count


def running_sum(rate):
    upto = (iota((BLOCK, BLOCK), 0) <= iota((BLOCK, BLOCK), 1)).astype(F32)
    return nn(rate, upto, precision=PRECISE)


def peer_copies(me, source, target, send_sem, recv_sem):
    @pl.loop(1, PEERS)
    def _(k):
        peer = lax.rem(me + k, PEERS)
        pltpu.make_async_remote_copy(
            src_ref=source.at[pl.ds(pl.multiple_of(peer * CAP, CAP), CAP)],
            dst_ref=target.at[pl.ds(pl.multiple_of(me * CAP, CAP), CAP)],
            send_sem=send_sem,
            recv_sem=recv_sem,
            device_id={"dp": peer // 2, "ctx": lax.rem(peer, 2)},
            device_id_type=MESH,
        ).start()

    own = pl.ds(pl.multiple_of(me * CAP, CAP), CAP)
    target[own, :] = source[own, :]


def block_copies(me, source, target, send_sem, recv_sem):
    single = source.shape[0] == 1

    @pl.loop(1, PEERS)
    def _(k):
        peer = lax.rem(me + k, PEERS)
        pltpu.make_async_remote_copy(
            src_ref=source.at[0 if single else peer],
            dst_ref=target.at[me],
            send_sem=send_sem,
            recv_sem=recv_sem,
            device_id={"dp": peer // 2, "ctx": lax.rem(peer, 2)},
            device_id_type=MESH,
        ).start()

    target[me] = source[0 if single else me]


def wait_blocks(ref, sem):
    view = ref.at[pl.ds(0, PEERS - 1)]
    pltpu.make_async_copy(view, view, sem).wait()


def quarter_picks(slot):
    at = iota((PEERS * QUART, ROWS), 0)
    first = (at % PEERS) * CAP + (at // PEERS) * 4
    return [as_bf16(slot == first + j) for j in range(4)]


def pack_steps(steps, picks, stage, out):
    total = None
    for j in range(4):
        pieces = [steps if i == j else jnp.zeros((HEADS, ROWS), BF16) for i in range(4)]
        term = nt(picks[j], jnp.concatenate(pieces, axis=0))
        total = term if total is None else total + term
    for i in range(QUART):
        stage[:, i, :] = total[PEERS * i : PEERS * i + PEERS]
    out[...] = stage[...].astype(BF16)


def unpack_steps(arrived, picks, stage):
    stage[...] = arrived[...].astype(F32)
    rows = jnp.concatenate([stage[:, i, :] for i in range(QUART)], axis=0).astype(BF16)
    total = None
    for j in range(4):
        term = tn(rows, picks[j])[HEADS * j : HEADS * j + HEADS]
        total = term if total is None else total + term
    return total


def wait_peers(ref, sem):
    view = ref.at[pl.ds(0, SLOTS - CAP)]
    pltpu.make_async_copy(view, view, sem).wait()


def layer_kernel(
    len_ref, place_ref, anchor_ref,
    x_ref, w_ref, r_ref, s_ref, cot_ref, dec_ref, bias_ref, skip_ref,
    y_ref, gx_ref, gw_ref, gr_ref, gs_ref, par_ref,
    snd_t, lnd_t, bck_t, ret_t, par_out, par_in, stage,
    snd_s, snd_x, lnd_s, lnd_x, bck_s, bck_x, ret_s, ret_x, edge_out, edge_in,
    perm_ref, pick_ref, xt_ref, bc_ref, u_ref, scale_ref, gain_ref,
    run_ref, wide_ref, step_ref, ent_ref, lev_ref, keep_ref, mask_ref, gram_ref, dgram_ref,
    dw_ref, dr_ref, dx_ref, yy_ref, xi_ref, xs_ref, kd_ref, gg_ref, dbc_ref,
    send_sem, recv_sem, back_send_sem, back_recv_sem, edge_send_sem, edge_recv_sem,
):
    dp, ctx = lax.axis_index("dp"), lax.axis_index("ctx")
    me = dp * 2 + ctx
    barrier = pltpu.get_barrier_semaphore()

    @pl.loop(1, PEERS)
    def _(k):
        peer = lax.rem(me + k, PEERS)
        pl.semaphore_signal(
            barrier, inc=1, device_id={"dp": peer // 2, "ctx": lax.rem(peer, 2)}, device_id_type=MESH
        )

    send_r = send_slot_row(place_ref[...])
    perm_ref[...] = as_bf16(iota((SLOTS, ROWS), 0) == send_r)
    send_picks = quarter_picks(send_r)
    pack_steps(s_ref[...], send_picks, stage, snd_t)
    snd_s[:, :STATE] = nn(perm_ref[...], w_ref[...]).astype(BF16)
    snd_s[:, STATE : 2 * STATE] = nn(perm_ref[...], r_ref[...]).astype(BF16)
    pl.semaphore_wait(barrier, PEERS - 1)
    block_copies(me, snd_t, lnd_t, send_sem.at[CHUNKS + 1], recv_sem.at[CHUNKS + 1])
    peer_copies(me, snd_s, lnd_s, send_sem.at[CHUNKS], recv_sem.at[CHUNKS])
    for k in range(CHUNKS):
        for half in range(CHUNK // 256):
            inside = slice(half * 256, half * 256 + 256)
            cols = slice(k * CHUNK + half * 256, k * CHUNK + half * 256 + 256)
            snd_x[k, :, inside] = nn(perm_ref[...], x_ref[:, cols]).astype(BF16)
        peer_copies(me, snd_x.at[k], lnd_x.at[k], send_sem.at[k], recv_sem.at[k])

    base = ctx * ROWS
    is_late = (ctx == 1).astype(F32)
    is_early = (ctx == 0).astype(F32)
    parts = (slice(0, BLOCK), slice(BLOCK, 2 * BLOCK))
    anchor_row, anchor_col = anchor_ref[...], int_column(anchor_ref[...])
    take_r = take_slot_row(anchor_col, anchor_row)
    pick_ref[...] = as_bf16(iota((SLOTS, ROWS), 0) == take_r)
    take_c = take_slot_col(anchor_col, anchor_row)
    pick = as_bf16(iota((ROWS, SLOTS), 1) == take_c)

    wait_peers(lnd_s, recv_sem.at[CHUNKS])
    wait_blocks(lnd_t, recv_sem.at[CHUNKS + 1])
    bc_ref[...] = nn(pick, lnd_s[...]).astype(BF16)
    take_picks = quarter_picks(take_r)
    u_ref[...] = unpack_steps(lnd_t, take_picks, stage) + column(bias_ref[...])
    u = u_ref[...]
    step = softplus(u)
    decay = -jnp.exp(column(dec_ref[...]))
    split_heads(gain_ref, jnp.broadcast_to(column(skip_ref[...]), (HEADS, BLOCK)))
    rate = decay * step
    split_heads(step_ref, step)
    keeps, runs = [], []
    for c in range(2):
        part = parts[c]
        first = base + c * BLOCK
        last = first + BLOCK - 1
        run = running_sum(rate[:, part])
        runs.append(run)
        split_heads(run_ref, run, part)
        pos = first + iota((1, BLOCK), 1)
        pos_col = first + iota((BLOCK, 1), 0)
        open_start = (starts_between(len_ref, jnp.full((1, BLOCK), first, jnp.int32), pos) == 0).astype(F32)
        open_end = (starts_between(len_ref, pos + 1, jnp.full((1, BLOCK), last, jnp.int32)) == 0).astype(F32)
        run_end = run[:, BLOCK - 1 :]
        split_heads(ent_ref, jnp.exp(run) * open_start, part)
        split_heads(lev_ref, jnp.exp(run_end - run) * step[:, part] * open_end, part)
        kept = jnp.exp(run_end) * open_start[:, BLOCK - 1 :]
        keeps.append(kept)
        split_heads(keep_ref, jnp.broadcast_to(kept, (HEADS, BLOCK)), part)
        crossing = starts_between(len_ref, pos + 1, pos_col)
        mask_ref[c] = jnp.where((pos_col >= pos) & (crossing == 0), 0.0, -1e30)
        tall = jnp.concatenate([run, jnp.zeros((128 - HEADS, BLOCK), F32)], axis=0).T
        for h in range(HEADS):
            wide_ref[h, part, :] = jnp.broadcast_to(tall[:, h : h + 1], (BLOCK, 128))
        gram_ref[c] = nt(bc_ref[part, STATE:], bc_ref[part, :STATE])
        dgram_ref[c] = jnp.zeros((BLOCK, BLOCK), F32)
        dw_ref[part, :] = jnp.zeros((BLOCK, STATE), F32)
        dr_ref[part, :] = jnp.zeros((BLOCK, STATE), F32)

    whole = jnp.concatenate([runs[0], runs[1] + runs[0][:, BLOCK - 1 :]], axis=1)
    pos = base + iota((1, ROWS), 1)
    open_end = (starts_between(len_ref, pos + 1, jnp.full((1, ROWS), base + ROWS - 1, jnp.int32)) == 0).astype(F32)
    open_start = (starts_between(len_ref, jnp.full((1, ROWS), base, jnp.int32), pos) == 0).astype(F32)
    leave_all = jnp.exp(whole[:, ROWS - 1 :] - whole) * step * open_end
    enter_all = jnp.exp(whole) * open_start
    split_heads(scale_ref, is_early * leave_all + is_late * enter_all)

    def scaled(h, values):
        four = [values[HEAD * i : HEAD * i + HEAD] * scale_ref[h + i] for i in range(4)]
        return split(jnp.concatenate(four, axis=0))

    def edge_copy(k):
        return pltpu.make_async_remote_copy(
            src_ref=edge_out.at[k],
            dst_ref=edge_in.at[k],
            send_sem=edge_send_sem.at[k],
            recv_sem=edge_recv_sem.at[k],
            device_id={"dp": dp, "ctx": 1 - ctx},
            device_id_type=MESH,
        )

    def open_chunk(k):
        wait_peers(lnd_x.at[k], recv_sem.at[k])
        for q in range(CHUNK // 256):
            inside = slice(q * 256, q * 256 + 256)
            rows = slice(k * CHUNK + q * 256, k * CHUNK + q * 256 + 256)
            xt_ref[rows, :] = tn(lnd_x[k, :, inside], pick_ref[...]).astype(BF16)
        head = k * CHUNK // HEAD

        @pl.when(ctx == 0)
        def _():
            for q in range(CHUNK // 256):
                rows = slice(k * CHUNK + q * 256, k * CHUNK + q * 256 + 256)
                values = scaled(head + 4 * q, xt_ref[rows, :].astype(F32))
                edge_out[k, q * 256 : q * 256 + 256, :] = both(nn, values, bc_ref[:, :STATE])

        @pl.when(ctx == 1)
        def _():
            for q in range(CHUNK // 256):
                rows = slice(k * CHUNK + q * 256, k * CHUNK + q * 256 + 256)
                values = scaled(head + 4 * q, cot_ref[:, rows].astype(F32).T)
                edge_out[k, q * 256 : q * 256 + 256, :] = both(nn, values, bc_ref[:, STATE:])

        edge_copy(k).start()

    def rows_of(ref, j, part):
        return jnp.concatenate(
            [jnp.broadcast_to(ref[2 * j + i, :, part], (HEAD, BLOCK)) for i in range(2)], axis=0
        )

    def pair(k, near):
        j = k * (CHUNK // 128) + near
        rows = pl.ds(pl.multiple_of(j * 128, 128), 128)
        edge = edge_in[k, pl.ds(pl.multiple_of(near * 128, 128), 128), :]
        x_t = [xt_ref[rows, part] for part in parts]
        x_f = [v.astype(F32) for v in x_t]
        d_n = [cot_ref[part, rows] for part in parts]
        d_f = [v.astype(F32).T for v in d_n]
        d_t = [v.astype(BF16) for v in d_f]
        gain = rows_of(gain_ref, j, slice(None))
        ent = [rows_of(ent_ref, j, part) for part in parts]
        lev = [rows_of(lev_ref, j, part) for part in parts]
        keep = [rows_of(keep_ref, j, part) for part in parts]
        w_t = [split(x_f[c] * lev[c]) for c in range(2)]
        v_t = [split(d_f[c] * ent[c]) for c in range(2)]
        state0 = edge * is_late
        state1 = both(nn, w_t[0], bc_ref[parts[0], :STATE]) + keep[0] * state0
        grad1 = edge * is_early
        grad0 = both(nn, v_t[1], bc_ref[parts[1], STATE:]) + keep[1] * grad1
        states, grads = (state0, state1), (grad0, grad1)
        upper = iota((128, BLOCK), 0) < HEAD
        for c in range(2):
            part = parts[c]
            y_parts, dx_parts = [], []
            for i in range(2):
                own = slice(HEAD * i, HEAD * i + HEAD)
                tall = wide_ref[2 * j + i, part, :]
                gap = jnp.concatenate([tall, tall], axis=1) - run_ref[2 * j + i, :, part]
                decayed = jnp.exp(gap + mask_ref[c]) * step_ref[2 * j + i, :, part]
                scores = split(gram_ref[c] * decayed)
                y_parts.append(both(nt, x_t[c][own], scores))
                dx_parts.append(both(nn, d_t[c][own], scores))
                only = jnp.where(upper if i == 0 else jnp.logical_not(upper), x_f[c], 0.0).astype(BF16)
                dgram_ref[c] += nn(d_n[c], only) * decayed
            state_b, grad_b = split(states[c]), split(grads[c])
            y_f = jnp.concatenate(y_parts, axis=0) + both(nt, state_b, bc_ref[part, STATE:]) * ent[c]
            dx_i = jnp.concatenate(dx_parts, axis=0)
            dx_s = both(nt, grad_b, bc_ref[part, :STATE]) * lev[c]
            yy, xi, xs, gg = d_f[c] * y_f, x_f[c] * dx_i, x_f[c] * dx_s, x_f[c] * d_f[c]
            kd = states[c] * grads[c]
            for i in range(2):
                own = slice(HEAD * i, HEAD * i + HEAD)
                one = 2 * j + i
                yy_ref[one, :, part] = jnp.sum(yy[own], axis=0, keepdims=True)
                xi_ref[one, :, part] = jnp.sum(xi[own], axis=0, keepdims=True)
                xs_ref[one, :, part] = jnp.sum(xs[own], axis=0, keepdims=True)
                gg_ref[one, :, part] = jnp.sum(gg[own], axis=0, keepdims=True)
                kd_ref[one, :, part] = jnp.sum(kd[own], axis=0, keepdims=True)
            y_ref[part, rows] = (y_f + gain * x_f[c]).T.astype(BF16)
            dx_ref[rows, part] = (dx_i + dx_s + gain * d_f[c]).astype(BF16)
            dw_ref[part, :] += both(tn, w_t[c], grad_b)
            dr_ref[part, :] += both(tn, v_t[c], state_b)

    def scan_chunk(k):
        edge_copy(k).wait()

        @pl.loop(0, CHUNK // 128)
        def _(near):
            pair(k, near)

        for q in range(CHUNK // 256):
            inside = slice(q * 256, q * 256 + 256)
            rows = slice(k * CHUNK + q * 256, k * CHUNK + q * 256 + 256)
            bck_x[k, :, inside] = nt(pick_ref[...], dx_ref[rows, :]).astype(BF16)
        peer_copies(me, bck_x.at[k], ret_x.at[k], back_send_sem.at[k], back_recv_sem.at[k])

    for k in range(CHUNKS):
        open_chunk(k)
        if k:
            scan_chunk(k - 1)
    scan_chunk(CHUNKS - 1)

    later = (iota((BLOCK, BLOCK), 0) >= iota((BLOCK, BLOCK), 1)).astype(F32)
    sooner = (iota((BLOCK, BLOCK), 0) < iota((BLOCK, BLOCK), 1)).astype(F32)
    drates = []
    yy, xi, xs = join_heads(yy_ref), join_heads(xi_ref), join_heads(xs_ref)
    for c in range(2):
        part = slice(c * BLOCK, c * BLOCK + BLOCK)
        dg = split(dgram_ref[c])
        write, read = bc_ref[part, :STATE], bc_ref[part, STATE:]
        dbc_ref[part, :STATE] = (dw_ref[part, :] + both(tn, dg, read)).astype(BF16)
        dbc_ref[part, STATE:] = (dr_ref[part, :] + both(nn, dg, write)).astype(BF16)
        through = keeps[c] * jnp.sum(join_heads(kd_ref, part), axis=1, keepdims=True)
        drate = (
            nn(yy[:, part] - xi[:, part], later, precision=PRECISE)
            + nn(xs[:, part], sooner, precision=PRECISE)
            + through
        )
        pos = base + c * BLOCK + iota((1, BLOCK), 1)
        drates.append(drate * (starts_between(len_ref, pos, pos) == 0).astype(F32))
    drate = jnp.concatenate(drates, axis=1)
    dstep = decay * drate + (xi + xs) / step
    du = dstep / (1.0 + jnp.exp(-u))
    lane, head = iota((HEADS, 128), 1), iota((HEADS, 128), 0)
    partial = (
        jnp.where(lane == HEADS + head, jnp.sum(drate * rate, axis=1, keepdims=True), 0.0)
        + jnp.where(lane == 2 * HEADS + head, jnp.sum(du, axis=1, keepdims=True), 0.0)
        + jnp.where(lane == 3 * HEADS + head, jnp.sum(join_heads(gg_ref), axis=1, keepdims=True), 0.0)
    )
    par_out[0] = jnp.sum(partial, axis=0, keepdims=True)
    block_copies(me, par_out, par_in, back_send_sem.at[CHUNKS + 2], back_recv_sem.at[CHUNKS + 2])
    bck_s[...] = nn(pick_ref[...], dbc_ref[...]).astype(BF16)
    peer_copies(me, bck_s, ret_s, back_send_sem.at[CHUNKS], back_recv_sem.at[CHUNKS])
    pack_steps(du.astype(BF16), quarter_picks(take_slot_row(int_column(anchor_ref[...]), anchor_ref[...])), stage, bck_t)
    block_copies(me, bck_t, ret_t, back_send_sem.at[CHUNKS + 1], back_recv_sem.at[CHUNKS + 1])

    perm = as_bf16(iota((ROWS, SLOTS), 1) == send_slot_col(int_column(place_ref[...])))
    for k in range(CHUNKS):
        wait_peers(ret_x.at[k], back_recv_sem.at[k])
        for q in range(CHUNK // 256):
            inside = slice(q * 256, q * 256 + 256)
            cols = slice(k * CHUNK + q * 256, k * CHUNK + q * 256 + 256)
            gx_ref[:, cols] = nn(perm, ret_x[k, :, inside]).astype(BF16)
    wait_peers(ret_s, back_recv_sem.at[CHUNKS])
    gw_ref[...] = nn(perm, ret_s[:, :STATE]).astype(BF16)
    gr_ref[...] = nn(perm, ret_s[:, STATE:]).astype(BF16)
    wait_blocks(par_in, back_recv_sem.at[CHUNKS + 2])
    total = jnp.sum(par_in[...], axis=0) * (1.0 / math.sqrt(ROWS * PEERS * HEAD))
    for k in range(3):
        par_ref[k : k + 1, :] = total[:, HEADS * (k + 1) : HEADS * (k + 2)]
    wait_blocks(ret_t, back_recv_sem.at[CHUNKS + 1])
    gs_ref[...] = unpack_steps(ret_t, quarter_picks(send_slot_row(place_ref[...])), stage).astype(BF16)
    for k in range(CHUNKS):
        wait_peers(snd_x.at[k], send_sem.at[k])
        wait_peers(bck_x.at[k], back_send_sem.at[k])
    wait_peers(snd_s, send_sem.at[CHUNKS])
    wait_peers(bck_s, back_send_sem.at[CHUNKS])
    wait_blocks(snd_t, send_sem.at[CHUNKS + 1])
    wait_blocks(bck_t, back_send_sem.at[CHUNKS + 1])
    wait_blocks(par_in, back_send_sem.at[CHUNKS + 2])


def finish_kernel(*refs):
    count = (len(refs) - 2) // 3
    groups = [refs[count * g : count * g + count] for g in range(3)]
    into_sem, out_sem = refs[-2:]
    pieces = []
    for source, target, middle in zip(*groups):
        parts = 4 if source.shape == (ROWS, WIDTH) else 1
        rows = source.shape[0] // parts
        for p in range(parts):
            part = pl.ds(p * rows, rows)
            n = len(pieces)
            pieces.append(
                (
                    pltpu.make_async_copy(source.at[part], middle.at[part], into_sem.at[n]),
                    pltpu.make_async_copy(middle.at[part], target.at[part], out_sem.at[n]),
                )
            )
    for first, _ in pieces:
        first.start()
    for first, second in pieces:
        first.wait()
        second.start()
    for _, second in pieces:
        second.wait()


def sds(shape, dtype):
    return jax.ShapeDtypeStruct(shape, dtype)


def vmem(n):
    return [pl.BlockSpec(memory_space=pltpu.VMEM)] * n


def per_device(
    head_inputs, write_vecs, read_vecs, step_raw, decay_log, step_bias, skip_gain,
    out_cotangent, rollout_lengths, plan_place, plan_anchor,
):
    small, large = (SLOTS, SMALL), (CHUNKS, SLOTS, CHUNK)
    per_head = pltpu.VMEM((HEADS, 1, ROWS), F32)
    square = pltpu.VMEM((2, BLOCK, BLOCK), F32)
    transfers = [pltpu.VMEM(shape, BF16) for _ in range(4) for shape in (small, large)]
    edges = [pltpu.VMEM((CHUNKS, CHUNK, STATE), F32)] * 2
    results = (
        sds((ROWS, WIDTH), BF16),
        sds((ROWS, WIDTH), BF16),
        sds((ROWS, STATE), BF16),
        sds((ROWS, STATE), BF16),
        sds((HEADS, ROWS), BF16),
        sds((3, HEADS), F32),
    )
    found = pl.pallas_call(
        layer_kernel,
        out_shape=results,
        in_specs=[pl.BlockSpec(memory_space=pltpu.SMEM)] + vmem(10),
        out_specs=tuple(vmem(6)),
        scratch_shapes=[
            *[pltpu.VMEM((PEERS, QUART, 128), BF16)] * 4,
            pltpu.VMEM((1, 1, 128), F32),
            pltpu.VMEM((PEERS, 1, 128), F32),
            pltpu.VMEM((PEERS, QUART, 128), F32),
            *transfers,
            *edges,
            pltpu.VMEM((SLOTS, ROWS), BF16),
            pltpu.VMEM((SLOTS, ROWS), BF16),
            pltpu.VMEM((WIDTH, ROWS), BF16),
            pltpu.VMEM((ROWS, 2 * STATE), BF16),
            pltpu.VMEM((HEADS, ROWS), F32),
            per_head,
            pltpu.VMEM((HEADS, 1, BLOCK), F32),
            per_head,
            pltpu.VMEM((HEADS, ROWS, 128), F32),
            per_head,
            per_head,
            per_head,
            per_head,
            square,
            square,
            square,
            pltpu.VMEM((ROWS, STATE), F32),
            pltpu.VMEM((ROWS, STATE), F32),
            pltpu.VMEM((WIDTH, ROWS), BF16),
            per_head,
            per_head,
            per_head,
            per_head,
            per_head,
            pltpu.VMEM((ROWS, 2 * STATE), BF16),
            pltpu.SemaphoreType.DMA((CHUNKS + 3,)),
            pltpu.SemaphoreType.DMA((CHUNKS + 3,)),
            pltpu.SemaphoreType.DMA((CHUNKS + 3,)),
            pltpu.SemaphoreType.DMA((CHUNKS + 3,)),
            pltpu.SemaphoreType.DMA((CHUNKS,)),
            pltpu.SemaphoreType.DMA((CHUNKS,)),
        ],
        compiler_params=pltpu.CompilerParams(
            collective_id=0, has_side_effects=True, vmem_limit_bytes=60 * 1024 * 1024
        ),
        name="layer",
    )(
        rollout_lengths, plan_place.reshape(1, ROWS), plan_anchor.reshape(1, ROWS),
        head_inputs, write_vecs, read_vecs, step_raw.T, out_cotangent,
        decay_log.reshape(1, HEADS), step_bias.reshape(1, HEADS), skip_gain.reshape(1, HEADS),
    )
    moved = pl.pallas_call(
        finish_kernel,
        out_shape=results[:5],
        in_specs=[pl.BlockSpec(memory_space=pl.ANY)] * 5,
        out_specs=tuple([pl.BlockSpec(memory_space=pl.ANY)] * 5),
        scratch_shapes=[pltpu.VMEM(r.shape, r.dtype) for r in results[:5]]
        + [pltpu.SemaphoreType.DMA((11,))] * 2,
        name="finish",
    )(*found[:5])
    layer_out, grad_x, grad_w, grad_r, grad_s = moved
    return (layer_out, grad_x, grad_w, grad_r, grad_s.T, found[5])


def solution(mesh):
    rows = P(("dp", "ctx"), "tp")
    return jax.shard_map(
        per_device,
        mesh=mesh,
        in_specs=(
            rows, rows, rows, rows, P("tp"), P("tp"), P("tp"), rows, P("dp", None), P(("dp", "ctx")), P(("dp", "ctx")),
        ),
        out_specs=(rows, rows, rows, rows, rows, P(None, "tp")),
        check_vma=False,
    )
```

```python
import math

import jax
import jax.numpy as jnp
from jax import lax
from jax.experimental import pallas as pl
from jax.experimental.pallas import tpu as pltpu
from jax.sharding import PartitionSpec as P

HEAD = 64
STATE = 256
BLOCK = 256
ROWS = 512
HEADS = 32
WIDTH = HEADS * HEAD
PEERS = 64
CAP = 16
SLOTS = PEERS * CAP
SMALL = 2 * STATE
QUART = CAP // 4
CHUNKS = 4
CHUNK = WIDTH // CHUNKS
MESH = pl.DeviceIdType.MESH
F32 = jnp.float32
BF16 = jnp.bfloat16
PRECISE = lax.Precision.HIGHEST


def nn(a, b, **kw):
    return lax.dot_general(a, b, (((1,), (0,)), ((), ())), preferred_element_type=F32, **kw)


def nt(a, b):
    return lax.dot_general(a, b, (((1,), (1,)), ((), ())), preferred_element_type=F32)


def tn(a, b):
    return lax.dot_general(a, b, (((0,), (0,)), ((), ())), preferred_element_type=F32)


def split(v):
    high = v.astype(BF16)
    return high, (v - high.astype(F32)).astype(BF16)


def both(product, a, b):
    if isinstance(a, tuple) and isinstance(b, tuple):
        return product(a[0], b[0]) + product(a[0], b[1]) + product(a[1], b[0])
    if isinstance(a, tuple):
        return product(a[0], b) + product(a[1], b)
    return product(a, b[0]) + product(a, b[1])


def iota(shape, dim):
    return lax.broadcasted_iota(jnp.int32, shape, dim)


def as_bf16(mask):
    return mask.astype(F32).astype(BF16)


def column(row):
    n = row.shape[1]
    return jnp.sum(jnp.where(iota((n, n), 0) == iota((n, n), 1), row, jnp.zeros((), row.dtype)), axis=1, keepdims=True)


def int_column(row):
    return column(row.astype(F32)).astype(jnp.int32)


def split_heads(ref, values, part=slice(None)):
    for h in range(HEADS):
        ref[h, :, part] = values[h : h + 1, :]


def join_heads(ref, part=slice(None)):
    return jnp.concatenate([ref[h, :, part] for h in range(HEADS)], axis=0)


def send_slot_row(place_row):
    target = lax.shift_right_logical(place_row, 9)
    ids = iota((PEERS, ROWS), 0)
    match = ids == target
    earlier = as_bf16(iota((ROWS, ROWS), 0) < iota((ROWS, ROWS), 1))
    before = nn(as_bf16(match), earlier)
    slot = jnp.sum(jnp.where(match, before + (ids * CAP).astype(F32), 0.0), axis=0, keepdims=True)
    return slot.astype(jnp.int32)


def send_slot_col(place_col):
    target = lax.shift_right_logical(place_col, 9)
    ids = iota((ROWS, PEERS), 1)
    match = ids == target
    earlier = as_bf16(iota((ROWS, ROWS), 1) < iota((ROWS, ROWS), 0))
    before = nn(earlier, as_bf16(match))
    slot = jnp.sum(jnp.where(match, before + (ids * CAP).astype(F32), 0.0), axis=1, keepdims=True)
    return slot.astype(jnp.int32)


def take_slot_row(anchor_col, anchor_row):
    source_row = lax.shift_right_logical(anchor_row, 9)
    same = lax.shift_right_logical(anchor_col, 9) == source_row
    before = jnp.where(same & (anchor_col < anchor_row), 1.0, 0.0)
    return source_row * CAP + jnp.sum(before, axis=0, keepdims=True).astype(jnp.int32)


def take_slot_col(anchor_col, anchor_row):
    source_col = lax.shift_right_logical(anchor_col, 9)
    same = source_col == lax.shift_right_logical(anchor_row, 9)
    before = jnp.where(same & (anchor_row < anchor_col), 1.0, 0.0)
    return source_col * CAP + jnp.sum(before, axis=1, keepdims=True).astype(jnp.int32)


def softplus(v):
    return jnp.maximum(v, 0.0) + jnp.log1p(jnp.exp(-jnp.abs(v)))


def starts_between(len_ref, low, high):
    first = len_ref[0, 0]
    second = first + len_ref[0, 1]
    count = jnp.zeros(jnp.broadcast_shapes(jnp.shape(low), jnp.shape(high)), F32)
    for bound in (0, first, second):
        count = count + jnp.where((bound >= low) & (bound <= high), 1.0, 0.0)
    return count


def running_sum(rate):
    upto = (iota((BLOCK, BLOCK), 0) <= iota((BLOCK, BLOCK), 1)).astype(F32)
    return nn(rate, upto, precision=PRECISE)


def peer_number(me, k):
    odd = lax.rem(k, 2)
    offset = odd * ((k + 1) // 2) + (1 - odd) * (PEERS - k // 2)
    return lax.rem(me + offset, PEERS)


def peer_copies(me, source, target, send_sem, recv_sem):
    @pl.loop(1, PEERS)
    def _(k):
        peer = peer_number(me, k)
        pltpu.make_async_remote_copy(
            src_ref=source.at[pl.ds(pl.multiple_of(peer * CAP, CAP), CAP)],
            dst_ref=target.at[pl.ds(pl.multiple_of(me * CAP, CAP), CAP)],
            send_sem=send_sem,
            recv_sem=recv_sem,
            device_id={"dp": peer // 2, "ctx": lax.rem(peer, 2)},
            device_id_type=MESH,
        ).start()

    own = pl.ds(pl.multiple_of(me * CAP, CAP), CAP)
    target[own, :] = source[own, :]


def block_copies(me, source, target, send_sem, recv_sem):
    single = source.shape[0] == 1

    @pl.loop(1, PEERS)
    def _(k):
        peer = peer_number(me, k)
        pltpu.make_async_remote_copy(
            src_ref=source.at[0 if single else peer],
            dst_ref=target.at[me],
            send_sem=send_sem,
            recv_sem=recv_sem,
            device_id={"dp": peer // 2, "ctx": lax.rem(peer, 2)},
            device_id_type=MESH,
        ).start()

    target[me] = source[0 if single else me]


def wait_blocks(ref, sem):
    view = ref.at[pl.ds(0, PEERS - 1)]
    pltpu.make_async_copy(view, view, sem).wait()


def quarter_picks(slot):
    at = iota((PEERS * QUART, ROWS), 0)
    first = (at % PEERS) * CAP + (at // PEERS) * 4
    return [as_bf16(slot == first + j) for j in range(4)]


def pack_steps(steps, picks, stage, out):
    total = None
    for j in range(4):
        pieces = [steps if i == j else jnp.zeros((HEADS, ROWS), BF16) for i in range(4)]
        term = nt(picks[j], jnp.concatenate(pieces, axis=0))
        total = term if total is None else total + term
    for i in range(QUART):
        stage[:, i, :] = total[PEERS * i : PEERS * i + PEERS]
    out[...] = stage[...].astype(BF16)


def unpack_steps(arrived, picks, stage):
    stage[...] = arrived[...].astype(F32)
    rows = jnp.concatenate([stage[:, i, :] for i in range(QUART)], axis=0).astype(BF16)
    total = None
    for j in range(4):
        term = tn(rows, picks[j])[HEADS * j : HEADS * j + HEADS]
        total = term if total is None else total + term
    return total


def wait_peers(ref, sem):
    view = ref.at[pl.ds(0, SLOTS - CAP)]
    pltpu.make_async_copy(view, view, sem).wait()


def layer_kernel(
    len_ref, place_ref, anchor_ref,
    x_ref, w_ref, r_ref, s_ref, cot_ref, dec_ref, bias_ref, skip_ref,
    y_ref, gx_ref, gw_ref, gr_ref, gs_ref, par_ref,
    snd_t, lnd_t, bck_t, ret_t, par_out, par_in, stage,
    snd_s, snd_x, lnd_s, lnd_x, bck_s, bck_x, ret_s, ret_x, edge_out, edge_in,
    perm_ref, pick_ref, xt_ref, bc_ref, u_ref, scale_ref, gain_ref,
    run_ref, wide_ref, step_ref, ent_ref, lev_ref, keep_ref, mask_ref, gram_ref, dgram_ref,
    dw_ref, dr_ref, dx_ref, yy_ref, xi_ref, xs_ref, kd_ref, gg_ref, dbc_ref,
    send_sem, recv_sem, back_send_sem, back_recv_sem, edge_send_sem, edge_recv_sem,
):
    dp, ctx = lax.axis_index("dp"), lax.axis_index("ctx")
    me = dp * 2 + ctx
    barrier = pltpu.get_barrier_semaphore()

    @pl.loop(1, PEERS)
    def _(k):
        peer = lax.rem(me + k, PEERS)
        pl.semaphore_signal(
            barrier, inc=1, device_id={"dp": peer // 2, "ctx": lax.rem(peer, 2)}, device_id_type=MESH
        )

    send_r = send_slot_row(place_ref[...])
    perm_ref[...] = as_bf16(iota((SLOTS, ROWS), 0) == send_r)
    send_picks = quarter_picks(send_r)
    pack_steps(s_ref[...], send_picks, stage, snd_t)
    snd_s[:, :STATE] = nn(perm_ref[...], w_ref[...]).astype(BF16)
    snd_s[:, STATE : 2 * STATE] = nn(perm_ref[...], r_ref[...]).astype(BF16)
    pl.semaphore_wait(barrier, PEERS - 1)
    block_copies(me, snd_t, lnd_t, send_sem.at[CHUNKS + 1], recv_sem.at[CHUNKS + 1])
    peer_copies(me, snd_s, lnd_s, send_sem.at[CHUNKS], recv_sem.at[CHUNKS])
    for k in range(CHUNKS):
        for half in range(CHUNK // 256):
            inside = slice(half * 256, half * 256 + 256)
            cols = slice(k * CHUNK + half * 256, k * CHUNK + half * 256 + 256)
            snd_x[k, :, inside] = nn(perm_ref[...], x_ref[:, cols]).astype(BF16)
        peer_copies(me, snd_x.at[k], lnd_x.at[k], send_sem.at[k], recv_sem.at[k])

    base = ctx * ROWS
    is_late = (ctx == 1).astype(F32)
    is_early = (ctx == 0).astype(F32)
    parts = (slice(0, BLOCK), slice(BLOCK, 2 * BLOCK))
    anchor_row, anchor_col = anchor_ref[...], int_column(anchor_ref[...])
    take_r = take_slot_row(anchor_col, anchor_row)
    pick_ref[...] = as_bf16(iota((SLOTS, ROWS), 0) == take_r)
    take_c = take_slot_col(anchor_col, anchor_row)
    pick = as_bf16(iota((ROWS, SLOTS), 1) == take_c)

    wait_peers(lnd_s, recv_sem.at[CHUNKS])
    wait_blocks(lnd_t, recv_sem.at[CHUNKS + 1])
    bc_ref[...] = nn(pick, lnd_s[...]).astype(BF16)
    take_picks = quarter_picks(take_r)
    u_ref[...] = unpack_steps(lnd_t, take_picks, stage) + column(bias_ref[...])
    u = u_ref[...]
    step = softplus(u)
    decay = -jnp.exp(column(dec_ref[...]))
    split_heads(gain_ref, jnp.broadcast_to(column(skip_ref[...]), (HEADS, BLOCK)))
    rate = decay * step
    split_heads(step_ref, step)
    keeps, runs = [], []
    for c in range(2):
        part = parts[c]
        first = base + c * BLOCK
        last = first + BLOCK - 1
        run = running_sum(rate[:, part])
        runs.append(run)
        split_heads(run_ref, run, part)
        pos = first + iota((1, BLOCK), 1)
        pos_col = first + iota((BLOCK, 1), 0)
        open_start = (starts_between(len_ref, jnp.full((1, BLOCK), first, jnp.int32), pos) == 0).astype(F32)
        open_end = (starts_between(len_ref, pos + 1, jnp.full((1, BLOCK), last, jnp.int32)) == 0).astype(F32)
        run_end = run[:, BLOCK - 1 :]
        split_heads(ent_ref, jnp.exp(run) * open_start, part)
        split_heads(lev_ref, jnp.exp(run_end - run) * step[:, part] * open_end, part)
        kept = jnp.exp(run_end) * open_start[:, BLOCK - 1 :]
        keeps.append(kept)
        split_heads(keep_ref, jnp.broadcast_to(kept, (HEADS, BLOCK)), part)
        crossing = starts_between(len_ref, pos + 1, pos_col)
        mask_ref[c] = jnp.where((pos_col >= pos) & (crossing == 0), 0.0, -1e30)
        tall = jnp.concatenate([run, jnp.zeros((128 - HEADS, BLOCK), F32)], axis=0).T
        for h in range(HEADS):
            wide_ref[h, part, :] = jnp.broadcast_to(tall[:, h : h + 1], (BLOCK, 128))
        gram_ref[c] = nt(bc_ref[part, STATE:], bc_ref[part, :STATE])
        dgram_ref[c] = jnp.zeros((BLOCK, BLOCK), F32)
        dw_ref[part, :] = jnp.zeros((BLOCK, STATE), F32)
        dr_ref[part, :] = jnp.zeros((BLOCK, STATE), F32)

    whole = jnp.concatenate([runs[0], runs[1] + runs[0][:, BLOCK - 1 :]], axis=1)
    pos = base + iota((1, ROWS), 1)
    open_end = (starts_between(len_ref, pos + 1, jnp.full((1, ROWS), base + ROWS - 1, jnp.int32)) == 0).astype(F32)
    open_start = (starts_between(len_ref, jnp.full((1, ROWS), base, jnp.int32), pos) == 0).astype(F32)
    leave_all = jnp.exp(whole[:, ROWS - 1 :] - whole) * step * open_end
    enter_all = jnp.exp(whole) * open_start
    split_heads(scale_ref, is_early * leave_all + is_late * enter_all)

    def scaled(h, values):
        four = [values[HEAD * i : HEAD * i + HEAD] * scale_ref[h + i] for i in range(4)]
        return split(jnp.concatenate(four, axis=0))

    def edge_copy(k):
        return pltpu.make_async_remote_copy(
            src_ref=edge_out.at[k],
            dst_ref=edge_in.at[k],
            send_sem=edge_send_sem.at[k],
            recv_sem=edge_recv_sem.at[k],
            device_id={"dp": dp, "ctx": 1 - ctx},
            device_id_type=MESH,
        )

    def open_chunk(k):
        wait_peers(lnd_x.at[k], recv_sem.at[k])
        for q in range(CHUNK // 256):
            inside = slice(q * 256, q * 256 + 256)
            rows = slice(k * CHUNK + q * 256, k * CHUNK + q * 256 + 256)
            xt_ref[rows, :] = tn(lnd_x[k, :, inside], pick_ref[...]).astype(BF16)
        head = k * CHUNK // HEAD

        @pl.when(ctx == 0)
        def _():
            for q in range(CHUNK // 256):
                rows = slice(k * CHUNK + q * 256, k * CHUNK + q * 256 + 256)
                values = scaled(head + 4 * q, xt_ref[rows, :].astype(F32))
                edge_out[k, q * 256 : q * 256 + 256, :] = both(nn, values, bc_ref[:, :STATE])

        @pl.when(ctx == 1)
        def _():
            for q in range(CHUNK // 256):
                rows = slice(k * CHUNK + q * 256, k * CHUNK + q * 256 + 256)
                values = scaled(head + 4 * q, cot_ref[:, rows].astype(F32).T)
                edge_out[k, q * 256 : q * 256 + 256, :] = both(nn, values, bc_ref[:, STATE:])

        edge_copy(k).start()

    def rows_of(ref, j, part):
        return jnp.concatenate(
            [jnp.broadcast_to(ref[2 * j + i, :, part], (HEAD, BLOCK)) for i in range(2)], axis=0
        )

    def pair(k, near):
        j = k * (CHUNK // 128) + near
        rows = pl.ds(pl.multiple_of(j * 128, 128), 128)
        edge = edge_in[k, pl.ds(pl.multiple_of(near * 128, 128), 128), :]
        x_t = [xt_ref[rows, part] for part in parts]
        x_f = [v.astype(F32) for v in x_t]
        d_n = [cot_ref[part, rows] for part in parts]
        d_f = [v.astype(F32).T for v in d_n]
        d_t = [v.astype(BF16) for v in d_f]
        gain = rows_of(gain_ref, j, slice(None))
        ent = [rows_of(ent_ref, j, part) for part in parts]
        lev = [rows_of(lev_ref, j, part) for part in parts]
        keep = [rows_of(keep_ref, j, part) for part in parts]
        w_t = [split(x_f[c] * lev[c]) for c in range(2)]
        v_t = [split(d_f[c] * ent[c]) for c in range(2)]
        state0 = edge * is_late
        state1 = both(nn, w_t[0], bc_ref[parts[0], :STATE]) + keep[0] * state0
        grad1 = edge * is_early
        grad0 = both(nn, v_t[1], bc_ref[parts[1], STATE:]) + keep[1] * grad1
        states, grads = (state0, state1), (grad0, grad1)
        upper = iota((128, BLOCK), 0) < HEAD
        for c in range(2):
            part = parts[c]
            y_parts, dx_parts = [], []
            for i in range(2):
                own = slice(HEAD * i, HEAD * i + HEAD)
                tall = wide_ref[2 * j + i, part, :]
                gap = jnp.concatenate([tall, tall], axis=1) - run_ref[2 * j + i, :, part]
                decayed = jnp.exp(gap + mask_ref[c]) * step_ref[2 * j + i, :, part]
                scores = split(gram_ref[c] * decayed)
                y_parts.append(both(nt, x_t[c][own], scores))
                dx_parts.append(both(nn, d_t[c][own], scores))
                only = jnp.where(upper if i == 0 else jnp.logical_not(upper), x_f[c], 0.0).astype(BF16)
                dgram_ref[c] += nn(d_n[c], only) * decayed
            state_b, grad_b = split(states[c]), split(grads[c])
            y_f = jnp.concatenate(y_parts, axis=0) + both(nt, state_b, bc_ref[part, STATE:]) * ent[c]
            dx_i = jnp.concatenate(dx_parts, axis=0)
            dx_s = both(nt, grad_b, bc_ref[part, :STATE]) * lev[c]
            yy, xi, xs, gg = d_f[c] * y_f, x_f[c] * dx_i, x_f[c] * dx_s, x_f[c] * d_f[c]
            kd = states[c] * grads[c]
            for i in range(2):
                own = slice(HEAD * i, HEAD * i + HEAD)
                one = 2 * j + i
                yy_ref[one, :, part] = jnp.sum(yy[own], axis=0, keepdims=True)
                xi_ref[one, :, part] = jnp.sum(xi[own], axis=0, keepdims=True)
                xs_ref[one, :, part] = jnp.sum(xs[own], axis=0, keepdims=True)
                gg_ref[one, :, part] = jnp.sum(gg[own], axis=0, keepdims=True)
                kd_ref[one, :, part] = jnp.sum(kd[own], axis=0, keepdims=True)
            y_ref[part, rows] = (y_f + gain * x_f[c]).T.astype(BF16)
            dx_ref[rows, part] = (dx_i + dx_s + gain * d_f[c]).astype(BF16)
            dw_ref[part, :] += both(tn, w_t[c], grad_b)
            dr_ref[part, :] += both(tn, v_t[c], state_b)

    def scan_chunk(k):
        edge_copy(k).wait()

        @pl.loop(0, CHUNK // 128)
        def _(near):
            pair(k, near)

        for q in range(CHUNK // 256):
            inside = slice(q * 256, q * 256 + 256)
            rows = slice(k * CHUNK + q * 256, k * CHUNK + q * 256 + 256)
            bck_x[k, :, inside] = nt(pick_ref[...], dx_ref[rows, :]).astype(BF16)
        peer_copies(me, bck_x.at[k], ret_x.at[k], back_send_sem.at[k], back_recv_sem.at[k])

    for k in range(CHUNKS):
        open_chunk(k)
        if k:
            scan_chunk(k - 1)
    scan_chunk(CHUNKS - 1)

    later = (iota((BLOCK, BLOCK), 0) >= iota((BLOCK, BLOCK), 1)).astype(F32)
    sooner = (iota((BLOCK, BLOCK), 0) < iota((BLOCK, BLOCK), 1)).astype(F32)
    drates = []
    yy, xi, xs = join_heads(yy_ref), join_heads(xi_ref), join_heads(xs_ref)
    for c in range(2):
        part = slice(c * BLOCK, c * BLOCK + BLOCK)
        dg = split(dgram_ref[c])
        write, read = bc_ref[part, :STATE], bc_ref[part, STATE:]
        dbc_ref[part, :STATE] = (dw_ref[part, :] + both(tn, dg, read)).astype(BF16)
        dbc_ref[part, STATE:] = (dr_ref[part, :] + both(nn, dg, write)).astype(BF16)
        through = keeps[c] * jnp.sum(join_heads(kd_ref, part), axis=1, keepdims=True)
        drate = (
            nn(yy[:, part] - xi[:, part], later, precision=PRECISE)
            + nn(xs[:, part], sooner, precision=PRECISE)
            + through
        )
        pos = base + c * BLOCK + iota((1, BLOCK), 1)
        drates.append(drate * (starts_between(len_ref, pos, pos) == 0).astype(F32))
    drate = jnp.concatenate(drates, axis=1)
    dstep = decay * drate + (xi + xs) / step
    du = dstep / (1.0 + jnp.exp(-u))
    lane, head = iota((HEADS, 128), 1), iota((HEADS, 128), 0)
    partial = (
        jnp.where(lane == HEADS + head, jnp.sum(drate * rate, axis=1, keepdims=True), 0.0)
        + jnp.where(lane == 2 * HEADS + head, jnp.sum(du, axis=1, keepdims=True), 0.0)
        + jnp.where(lane == 3 * HEADS + head, jnp.sum(join_heads(gg_ref), axis=1, keepdims=True), 0.0)
    )
    par_out[0] = jnp.sum(partial, axis=0, keepdims=True)
    block_copies(me, par_out, par_in, back_send_sem.at[CHUNKS + 2], back_recv_sem.at[CHUNKS + 2])
    bck_s[...] = nn(pick_ref[...], dbc_ref[...]).astype(BF16)
    peer_copies(me, bck_s, ret_s, back_send_sem.at[CHUNKS], back_recv_sem.at[CHUNKS])
    pack_steps(du.astype(BF16), quarter_picks(take_slot_row(int_column(anchor_ref[...]), anchor_ref[...])), stage, bck_t)
    block_copies(me, bck_t, ret_t, back_send_sem.at[CHUNKS + 1], back_recv_sem.at[CHUNKS + 1])

    perm = as_bf16(iota((ROWS, SLOTS), 1) == send_slot_col(int_column(place_ref[...])))
    for k in range(CHUNKS):
        wait_peers(ret_x.at[k], back_recv_sem.at[k])
        for q in range(CHUNK // 256):
            inside = slice(q * 256, q * 256 + 256)
            cols = slice(k * CHUNK + q * 256, k * CHUNK + q * 256 + 256)
            gx_ref[:, cols] = nn(perm, ret_x[k, :, inside]).astype(BF16)
    wait_peers(ret_s, back_recv_sem.at[CHUNKS])
    gw_ref[...] = nn(perm, ret_s[:, :STATE]).astype(BF16)
    gr_ref[...] = nn(perm, ret_s[:, STATE:]).astype(BF16)
    wait_blocks(par_in, back_recv_sem.at[CHUNKS + 2])
    total = jnp.sum(par_in[...], axis=0) * (1.0 / math.sqrt(ROWS * PEERS * HEAD))
    for k in range(3):
        par_ref[k : k + 1, :] = total[:, HEADS * (k + 1) : HEADS * (k + 2)]
    wait_blocks(ret_t, back_recv_sem.at[CHUNKS + 1])
    gs_ref[...] = unpack_steps(ret_t, quarter_picks(send_slot_row(place_ref[...])), stage).astype(BF16)
    for k in range(CHUNKS):
        wait_peers(snd_x.at[k], send_sem.at[k])
        wait_peers(bck_x.at[k], back_send_sem.at[k])
    wait_peers(snd_s, send_sem.at[CHUNKS])
    wait_peers(bck_s, back_send_sem.at[CHUNKS])
    wait_blocks(snd_t, send_sem.at[CHUNKS + 1])
    wait_blocks(bck_t, back_send_sem.at[CHUNKS + 1])
    wait_blocks(par_in, back_send_sem.at[CHUNKS + 2])


def finish_kernel(*refs):
    count = (len(refs) - 2) // 3
    groups = [refs[count * g : count * g + count] for g in range(3)]
    into_sem, out_sem = refs[-2:]
    pieces = []
    for source, target, middle in zip(*groups):
        parts = 4 if source.shape == (ROWS, WIDTH) else 1
        rows = source.shape[0] // parts
        for p in range(parts):
            part = pl.ds(p * rows, rows)
            n = len(pieces)
            pieces.append(
                (
                    pltpu.make_async_copy(source.at[part], middle.at[part], into_sem.at[n]),
                    pltpu.make_async_copy(middle.at[part], target.at[part], out_sem.at[n]),
                )
            )
    for first, _ in pieces:
        first.start()
    for first, second in pieces:
        first.wait()
        second.start()
    for _, second in pieces:
        second.wait()


def sds(shape, dtype):
    return jax.ShapeDtypeStruct(shape, dtype)


def vmem(n):
    return [pl.BlockSpec(memory_space=pltpu.VMEM)] * n


def per_device(
    head_inputs, write_vecs, read_vecs, step_raw, decay_log, step_bias, skip_gain,
    out_cotangent, rollout_lengths, plan_place, plan_anchor,
):
    small, large = (SLOTS, SMALL), (CHUNKS, SLOTS, CHUNK)
    per_head = pltpu.VMEM((HEADS, 1, ROWS), F32)
    square = pltpu.VMEM((2, BLOCK, BLOCK), F32)
    transfers = [pltpu.VMEM(shape, BF16) for _ in range(4) for shape in (small, large)]
    edges = [pltpu.VMEM((CHUNKS, CHUNK, STATE), F32)] * 2
    results = (
        sds((ROWS, WIDTH), BF16),
        sds((ROWS, WIDTH), BF16),
        sds((ROWS, STATE), BF16),
        sds((ROWS, STATE), BF16),
        sds((HEADS, ROWS), BF16),
        sds((3, HEADS), F32),
    )
    found = pl.pallas_call(
        layer_kernel,
        out_shape=results,
        in_specs=[pl.BlockSpec(memory_space=pltpu.SMEM)] + vmem(10),
        out_specs=tuple(vmem(6)),
        scratch_shapes=[
            *[pltpu.VMEM((PEERS, QUART, 128), BF16)] * 4,
            pltpu.VMEM((1, 1, 128), F32),
            pltpu.VMEM((PEERS, 1, 128), F32),
            pltpu.VMEM((PEERS, QUART, 128), F32),
            *transfers,
            *edges,
            pltpu.VMEM((SLOTS, ROWS), BF16),
            pltpu.VMEM((SLOTS, ROWS), BF16),
            pltpu.VMEM((WIDTH, ROWS), BF16),
            pltpu.VMEM((ROWS, 2 * STATE), BF16),
            pltpu.VMEM((HEADS, ROWS), F32),
            per_head,
            pltpu.VMEM((HEADS, 1, BLOCK), F32),
            per_head,
            pltpu.VMEM((HEADS, ROWS, 128), F32),
            per_head,
            per_head,
            per_head,
            per_head,
            square,
            square,
            square,
            pltpu.VMEM((ROWS, STATE), F32),
            pltpu.VMEM((ROWS, STATE), F32),
            pltpu.VMEM((WIDTH, ROWS), BF16),
            per_head,
            per_head,
            per_head,
            per_head,
            per_head,
            pltpu.VMEM((ROWS, 2 * STATE), BF16),
            pltpu.SemaphoreType.DMA((CHUNKS + 3,)),
            pltpu.SemaphoreType.DMA((CHUNKS + 3,)),
            pltpu.SemaphoreType.DMA((CHUNKS + 3,)),
            pltpu.SemaphoreType.DMA((CHUNKS + 3,)),
            pltpu.SemaphoreType.DMA((CHUNKS,)),
            pltpu.SemaphoreType.DMA((CHUNKS,)),
        ],
        compiler_params=pltpu.CompilerParams(
            collective_id=0, has_side_effects=True, vmem_limit_bytes=60 * 1024 * 1024
        ),
        name="layer",
    )(
        rollout_lengths, plan_place.reshape(1, ROWS), plan_anchor.reshape(1, ROWS),
        head_inputs, write_vecs, read_vecs, step_raw.T, out_cotangent,
        decay_log.reshape(1, HEADS), step_bias.reshape(1, HEADS), skip_gain.reshape(1, HEADS),
    )
    moved = pl.pallas_call(
        finish_kernel,
        out_shape=results[:5],
        in_specs=[pl.BlockSpec(memory_space=pl.ANY)] * 5,
        out_specs=tuple([pl.BlockSpec(memory_space=pl.ANY)] * 5),
        scratch_shapes=[pltpu.VMEM(r.shape, r.dtype) for r in results[:5]]
        + [pltpu.SemaphoreType.DMA((11,))] * 2,
        name="finish",
    )(*found[:5])
    layer_out, grad_x, grad_w, grad_r, grad_s = moved
    return (layer_out, grad_x, grad_w, grad_r, grad_s.T, found[5])


def solution(mesh):
    rows = P(("dp", "ctx"), "tp")
    return jax.shard_map(
        per_device,
        mesh=mesh,
        in_specs=(
            rows, rows, rows, rows, P("tp"), P("tp"), P("tp"), rows, P("dp", None), P(("dp", "ctx")), P(("dp", "ctx")),
        ),
        out_specs=(rows, rows, rows, rows, rows, P(None, "tp")),
        check_vma=False,
    )
```
